256 devices in a mesh: gr: 32 (over z_hi, y, core), gc: 8 (over x, z_lo).
Axes of the slice: x: 4, y: 4, z: 8 (z_hi: 4, z_lo: 2; z = z_hi * 2 + z_lo), core: 2. Of those that a mesh axis runs over, the one named last changes fastest.
Arguments:
- counts: int32 [40960, 16384], P('gr', 'gc'), may hold values from 0 to 1600
- row_ids: int32 [40960], P('gr'), may hold values from 0 to 40959, each once
- col_ids: int32 [16384], P('gc'), may hold values from 0 to 16383, each once
- row_marginal: int32 [40960], replicated, may hold values from 50000 to 999999
- col_marginal: int32 [16384], replicated, may hold values from 50000 to 999999
- row_emb: float32 [40960, 256], P(('gr', 'gc')), may hold values from -1.5 to 1.5
- row_acc: float32 [40960, 256], P(('gr', 'gc')), may hold values from 0.5 to 20
- col_emb: float32 [16384, 256], P(('gc', 'gr')), may hold values from -1.5 to 1.5
- col_acc: float32 [16384, 256], P(('gc', 'gr')), may hold values from 0.5 to 20
Outputs:
- row_new: float32 [40960, 256], P(('gr', 'gc'))
- row_acc_new: float32 [40960, 256], P(('gr', 'gc'))
- col_new: float32 [16384, 256], P(('gc', 'gr'))
- col_acc_new: float32 [16384, 256], P(('gc', 'gr'))
The draws below stay inside these ranges and needn't reach their ends.
Inputs may be any that keep to these rules, and one draw needn't show every extreme that they name: `row_ids`: a permutation of the row ids. `col_ids`: a permutation of the column ids.
All inputs are finite; a program needn't handle non-finite values.
Results may differ from the reference program's by a relative error of at most 0.0082.
Values may be sent and summed in bfloat16 or wider, within the bound.
A program may use at most 64 MiB of HBM per device.

```python
import math
import jax
import jax.numpy as jnp
from jax import lax

K = 256
ROWS = 40960
COLS = 16384


def draw_counts(key, part):
    key = jax.random.fold_in(key, 11)
    first, second = jax.random.split(key, 2)
    expo = jax.random.randint(first, (ROWS, COLS), 0, 12)
    upper = jnp.left_shift(jnp.ones((ROWS, COLS), jnp.int32), expo)
    upper = jnp.minimum(upper, 1601)
    values = jax.random.randint(second, (ROWS, COLS), 0, upper)
    return values.at[0, 0].set(1600).astype(jnp.int32)


def place_ends(entries, stream_key, least, largest):
    index_at = [jax.random.randint(jax.random.fold_in(stream_key, axis), (), 0, length) for axis, length in enumerate(entries.shape)]
    widest = entries.shape.index(max(entries.shape))
    next_to = index_at[:widest] + [(index_at[widest] + 1) % entries.shape[widest]] + index_at[widest + 1:]
    return entries.at[tuple(index_at)].set(least).at[tuple(next_to)].set(largest)


def level_of(key, shape, cuts, low, largest):
    gain, own = 1.0, jax.random.fold_in(key, 6)
    for axis_at, shards_of in cuts:
        steps = jnp.exp(jax.random.uniform(jax.random.fold_in(own, axis_at), (shards_of,), jnp.float32, low / len(cuts), largest / len(cuts)))
        gain = gain * jnp.repeat(steps, shape[axis_at] // shards_of).reshape([-1 if axis == axis_at else 1 for axis in range(len(shape))])
    return gain


def gaussian(rng, extent, spread, most, cuts=(), held_as=jnp.bfloat16):
    drawn = jax.random.normal(rng, extent, jnp.float32) * spread
    if len(cuts) > 0:
        drawn = level_of(rng, extent, cuts, -0.22, 0.18) * drawn
    return jnp.clip(drawn, min=-most, max=most).astype(held_as)


def setup_inputs(seed: int = 0) -> dict:
    arg_keys = jax.random.split(jax.random.key(seed), 10)
    counts = draw_counts(jax.random.fold_in(arg_keys[9], 71), 0)
    row_ids = jax.random.permutation(arg_keys[1], ROWS).astype(jnp.int32)
    col_ids = jax.random.permutation(arg_keys[2], COLS).astype(jnp.int32)
    row_marginal = place_ends(jax.random.randint(arg_keys[3], (ROWS,), 50000, 1000000), jax.random.fold_in(arg_keys[3], 1), 50000, 999999).astype(jnp.int32)
    col_marginal = place_ends(jax.random.randint(arg_keys[4], (COLS,), 50000, 1000000), jax.random.fold_in(arg_keys[4], 1), 50000, 999999).astype(jnp.int32)
    row_emb = gaussian(arg_keys[5], (ROWS, K), 0.25, 1.5, ((0, 256),), jnp.float32)
    row_acc = jnp.clip(jnp.exp(math.log(20.0) - 3.6888795 * jax.random.uniform(arg_keys[6], (ROWS, K), jnp.float32) ** level_of(arg_keys[6], (ROWS, K), ((0, 256),), -0.2, 0.2)), 0.5, 20.0)
    col_emb = gaussian(arg_keys[7], (COLS, K), 0.25, 1.5, ((0, 256),), jnp.float32)
    col_acc = jnp.clip(jnp.exp(math.log(20.0) - 3.6888795 * jax.random.uniform(arg_keys[8], (COLS, K), jnp.float32) ** level_of(arg_keys[8], (COLS, K), ((0, 256),), -0.2, 0.2)), 0.5, 20.0)
    return {"counts": counts, "row_ids": row_ids, "col_ids": col_ids, "row_marginal": row_marginal, "col_marginal": col_marginal, "row_emb": row_emb, "row_acc": row_acc, "col_emb": col_emb, "col_acc": col_acc}


learn_rate = 0.5

def block_grad(cnt, row_log, col_log, log_total, rows_half, cols_half, factor):
    score = lax.dot_general(rows_half, cols_half, (((1,), (1,)), ((), ())), preferred_element_type=jnp.float32)
    pmi = jnp.log(jnp.maximum(cnt, 1).astype(jnp.float32)) + log_total - row_log[:, None] - col_log[None, :]
    diff = score - pmi
    confid = 0.1 + 0.25 * jnp.sqrt(cnt.astype(jnp.float32))
    grad = jnp.where(cnt > 0, confid * diff, jax.nn.sigmoid(diff)) * factor
    grad_half = grad.astype(jnp.bfloat16)
    row_part = jnp.dot(grad_half, cols_half, preferred_element_type=jnp.float32)
    col_part = lax.dot_general(grad_half, rows_half, (((0,), (0,)), ((), ())), preferred_element_type=jnp.float32)
    return (row_part, col_part)

def adagrad(emb, acc, grad):
    acc_new = acc + grad * grad
    return (emb - learn_rate * grad / jnp.sqrt(acc_new), acc_new)

def reference(counts, row_ids, col_ids, row_marginal, col_marginal, row_emb, row_acc, col_emb, col_acc):
    log_total = jnp.log(jnp.sum(row_marginal.astype(jnp.float32)))
    row_log = jnp.log(row_marginal[row_ids].astype(jnp.float32))
    col_log = jnp.log(col_marginal[col_ids].astype(jnp.float32))
    row_half = row_emb.astype(jnp.bfloat16)
    col_half = col_emb.astype(jnp.bfloat16)
    factor = 1.0 / math.sqrt(COLS)
    blk = math.gcd(ROWS, 512)
    nblocks = ROWS // blk
    cnt_blocks = counts.reshape(nblocks, blk, COLS)
    half_blocks = row_half.reshape(nblocks, blk, K)
    log_blocks = row_log.reshape(nblocks, blk)

    def step(col_grad, items):
        cnt, rows_half, rlog = items
        row_part, col_part = block_grad(cnt, rlog, col_log, log_total, rows_half, col_half, factor)
        return (col_grad + col_part, row_part)
    col_grad, row_parts = lax.scan(step, jnp.zeros((COLS, K), jnp.float32), (cnt_blocks, half_blocks, log_blocks))
    row_grad = row_parts.reshape(ROWS, K)
    row_new, row_acc_new = adagrad(row_emb, row_acc, row_grad)
    col_new, col_acc_new = adagrad(col_emb, col_acc, col_grad)
    return (row_new, row_acc_new, col_new, col_acc_new)
```

```python
import functools

import jax
import jax.numpy as jnp
from jax import lax
from jax.experimental import pallas as pl
from jax.experimental.pallas import tpu as pltpu
from jax.sharding import PartitionSpec as P

F32 = jnp.float32
BF16 = jnp.bfloat16
MESH = pl.DeviceIdType.MESH

LEARN_RATE = 0.5
K = 256
NX, NZL = 4, 2
NZH, NY, NC = 4, 4, 2
RB = 160
CB = 64
XB = RB * NZL
QB = NZH * NC * CB
ROWS = NX * XB
COLS = NY * QB
SUB = 16
Q_STEPS = (1, 2, 3, 0)
X_FIRST = (0, 1, 3, 2)
X_LAST = (2, 1, 3, 0)
N_SEMS = 64


def lookup(table, ids):
    high = lax.shift_right_logical(ids, 7)
    low = ids & 127
    n_high, n = table.shape[0], ids.shape[1]
    hot = (lax.broadcasted_iota(jnp.int32, (n_high, n), 0) == high).astype(F32).astype(BF16)
    digits = [
        lax.shift_right_logical(table, 16),
        lax.shift_right_logical(table, 8) & 255,
        table & 255,
    ]
    parts = [
        jnp.dot(d.astype(F32).T.astype(BF16), hot, preferred_element_type=F32) for d in digits
    ]
    whole = parts[0] * 65536.0 + parts[1] * 256.0 + parts[2]
    mine = lax.broadcasted_iota(jnp.int32, (128, n), 0) == low
    return jnp.log(jnp.sum(jnp.where(mine, whole, 0.0), axis=0, keepdims=True))


def kernel(
    cnt_hbm, rid_hbm, cid_hbm, rmar_hbm, cmar_hbm, remb_hbm, racc_hbm, cemb_hbm, cacc_hbm,
    rnew_ref, raccn_ref, cnew_ref, caccn_ref,
    cnt, rid, cid, rmar, cmar, remb, racc, cemb, cacc,
    rows, rows_t, cols, cols_t, row_term, col_term,
    s_ref, g_ref, row_part, col_tmp, col_part, q_sum,
    ex_s, ex_r, y2p_s, y2p_r, y2m_s, y2m_r, y3p_s, y3p_r, y3m_s, y3m_r,
    z2p_s, z2p_r, z2m_s, z2m_r, z3p_s, z3p_r, z3m_s, z3m_r,
    x2p_s, x2p_r, x2m_s, x2m_r, x3p_s, x3p_r, x3m_s, x3m_r, w_s, w_r,
    local_sem, send_sem, recv_sem,
):
    gr = lax.axis_index("gr")
    gc = lax.axis_index("gc")
    c = lax.rem(gr, NC)
    y = lax.rem(gr // NC, NY)
    zh = gr // (NC * NY)
    zl = lax.rem(gc, NZL)
    x = gc // NZL

    def at(dx=0, dzl=0, dzh=0, dy=0, dc=0):
        g = (lax.rem(zh + dzh, NZH) * NY + lax.rem(y + dy, NY)) * NC + lax.rem(c + dc, NC)
        k = lax.rem(x + dx, NX) * NZL + lax.rem(zl + dzl, NZL)
        return (g, k)

    ZP, ZM = at(dzh=1), at(dzh=3)
    YP, YM = at(dy=1), at(dy=3)
    XP, XM = at(dx=1), at(dx=3)
    CO, LO = at(dc=1), at(dzl=1)
    neighbours = (ZP, ZM, YP, YM, XP, XM, CO, LO)

    loads = []

    def load(src, dst):
        cp = pltpu.make_async_copy(src, dst, local_sem.at[len(loads)])
        cp.start()
        loads.append(cp)
        return cp

    l_remb, l_cemb = load(remb_hbm, remb), load(cemb_hbm, cemb)
    barrier = pltpu.get_barrier_semaphore()
    for n in neighbours:
        pl.semaphore_signal(barrier, inc=1, device_id=n, device_id_type=MESH)
    l_ids = [load(rid_hbm, rid), load(cid_hbm, cid), load(rmar_hbm, rmar), load(cmar_hbm, cmar)]
    l_cnt = [
        load(cnt_hbm.at[pl.ds(i * XB, XB)], cnt.at[pl.ds(i * XB, XB)]) for i in range(NX)
    ]
    l_acc = [load(racc_hbm, racc), load(cacc_hbm, cacc)]

    copies = []

    def send(src, dst, target):
        i = len(copies)
        cp = pltpu.make_async_remote_copy(
            src_ref=src, dst_ref=dst, send_sem=send_sem.at[i], recv_sem=recv_sem.at[i],
            device_id=target, device_id_type=MESH,
        )
        cp.start()
        copies.append(cp)
        return cp

    def zz(d):
        return lax.rem(zh + d, NZH)

    def yy(d):
        return lax.rem(y + d, NY)

    def xx(d):
        return lax.rem(x + d, NX)

    def same(ref, target):
        return send(ref, ref, target)

    l_remb.wait()
    rows[x, zl] = (remb[...] * 0.5).astype(BF16)
    l_cemb.wait()
    cols[y, zh, c] = cemb[...].astype(BF16)
    pl.semaphore_wait(barrier, len(neighbours))

    own_r, own_c = rows.at[x, zl], cols.at[y, zh, c]
    r_lo = same(own_r, LO)
    r_p0, r_m0 = same(own_r, XP), same(own_r, XM)
    c_zp, c_zm = same(own_c, ZP), same(own_c, ZM)
    c_yp, c_ym = {0: same(own_c, YP)}, {0: same(own_c, YM)}

    for cp in l_ids:
        cp.wait()
    col_log = lookup(cmar[...], cid[...])
    col_term[...] = jnp.broadcast_to(0.5 * col_log, col_term.shape)
    r_lo.wait_recv()
    other_r = rows.at[x, 1 - zl]
    r_p1, r_m1 = same(other_r, XP), same(other_r, XM)
    c_zp.wait_recv()
    c_zfp = same(cols.at[y, zz(3), c, pl.ds(0, 32)], ZP)
    c_yp[3], c_ym[3] = same(cols.at[y, zz(3), c], YP), same(cols.at[y, zz(3), c], YM)
    c_zm.wait_recv()
    c_zfm = same(cols.at[y, zz(1), c, pl.ds(32, 32)], ZM)
    c_yp[1], c_ym[1] = same(cols.at[y, zz(1), c], YP), same(cols.at[y, zz(1), c], YM)
    c_yp[0].wait_recv()
    c_yfp = {0: same(cols.at[yy(3), zh, c], YP)}
    row_log = lookup(rmar[...], rid[...])
    log_total = jnp.log(jnp.sum(rmar[...].astype(F32)))
    row_vec = 0.5 * (row_log - log_total)
    for b in range(ROWS // 128):
        piece = jnp.broadcast_to(row_vec[:, b * 128 : (b + 1) * 128], (128, 128))
        row_term[b * 128 : (b + 1) * 128, :] = piece.T
    c_zfp.wait_recv()
    c_zfm.wait_recv()
    c_yp[2], c_ym[2] = same(cols.at[y, zz(2), c], YP), same(cols.at[y, zz(2), c], YM)
    core = {0: same(cols.at[y, :, c], CO)}
    r_p0.wait_recv()
    r_fp = same(rows.at[xx(3), zl], XP)
    c_ym[3].wait_recv()
    c_yfm = {3: same(cols.at[yy(1), zz(3), c], YM)}
    c_ym[1].wait_recv()
    c_yfm[1] = same(cols.at[yy(1), zz(1), c], YM)
    r_m1.wait_recv()
    r_fm = same(rows.at[xx(1), 1 - zl], XM)
    c_yp[2].wait_recv()
    c_yfp[2] = same(cols.at[yy(3), zz(2), c], YP)
    c_ym[0].wait_recv()
    c_ym[2].wait_recv()
    core[1] = same(cols.at[yy(1), :, c], CO)
    c_yp[1].wait_recv()
    c_yp[3].wait_recv()
    core[3] = same(cols.at[yy(3), :, c], CO)
    r_m0.wait_recv()
    r_p1.wait_recv()
    for cp in (c_yfp[0], c_yfm[3], c_yfm[1], c_yfp[2]):
        cp.wait_recv()
    core[2] = same(cols.at[yy(2), :, c], CO)
    r_fp.wait_recv()
    r_fm.wait_recv()
    for i in range(NX):
        rows_t[:, i * XB : (i + 1) * XB] = rows[i].reshape(XB, K).T
    for d in Q_STEPS:
        core[d].wait_recv()
        cols_t[yy(d)] = cols[yy(d)].reshape(QB, K).T
    for cp in l_cnt:
        cp.wait()

    def score(s, i):
        q, dx = yy(Q_STEPS[s]), x_order(s)[i]
        s_ref[i % 2] = jnp.dot(
            rows[xx(dx)].reshape(XB, K), cols_t[q], preferred_element_type=F32
        )

    def x_order(s):
        return X_LAST if s == NY - 1 else X_FIRST

    def elem(s, i):
        q, r_at = yy(Q_STEPS[s]), pl.multiple_of(xx(x_order(s)[i]) * XB, XB)
        for z in range(NZH):
            c_at = pl.multiple_of(z * QB + q * 128, 128)
            c_row = col_term[:, pl.ds(c_at, 128)]
            for u in range(XB // SUB):
                at_u = pl.ds(pl.multiple_of(r_at + u * SUB, SUB), SUB)
                n = cnt[at_u, pl.ds(c_at, 128)]
                m = jnp.maximum(n, 1).astype(F32)
                inv = lax.rsqrt(m)
                half = (
                    s_ref[i % 2, u * SUB : (u + 1) * SUB, z * 128 : (z + 1) * 128] + jnp.log(inv)
                ) + (row_term[at_u, :] + c_row)
                g = jnp.where(n > 0, (m * inv + 0.4) * half, jnp.tanh(half) + 1.0)
                g_ref[s % 2, at_u, z * 128 : (z + 1) * 128] = g.astype(BF16)

    def row_grad(s, i):
        q, at_x = yy(Q_STEPS[s]), xx(x_order(s)[i])
        r_at = pl.multiple_of(at_x * XB, XB)
        part = jnp.dot(
            g_ref[s % 2, pl.ds(r_at, XB), :], cols[q].reshape(QB, K), preferred_element_type=F32
        ).reshape(NZL, RB, K)
        if s == 0:
            row_part[at_x] = part
        else:
            row_part[at_x] += part

    def col_grad(s):
        t = jnp.dot(rows_t[...], g_ref[s % 2], preferred_element_type=F32)
        col_tmp[s % 2] = t.T.reshape(NZH, NC, CB, K)
        ex_s[s] = col_tmp[s % 2, :, 1 - c].astype(BF16)
        col_part[s] = col_tmp[s % 2, :, c]
        return send(ex_s.at[s], ex_r.at[s], CO)

    ex, hop = {}, {}

    def y_far():
        ex[1].wait_recv()
        total = col_part[1] + ex_r[1].astype(F32)
        y2p_s[...] = total[0:2].astype(BF16)
        y2m_s[...] = total[2:4].astype(BF16)
        hop["y2p"] = send(y2p_s, y2p_r, YP)
        hop["y2m"] = send(y2m_s, y2m_r, YM)

    def y_up():
        ex[0].wait_recv()
        hop["y2p"].wait_recv()
        total = col_part[0] + ex_r[0].astype(F32)
        y3p_s[0:2] = (total[0:2] + y2p_r[...].astype(F32)).astype(BF16)
        y3p_s[2:4] = total[2:4].astype(BF16)
        hop["y3p"] = send(y3p_s, y3p_r, YP)

    def y_down():
        ex[2].wait_recv()
        hop["y2m"].wait_recv()
        total = col_part[2] + ex_r[2].astype(F32)
        y3m_s[0:2] = total[0:2].astype(BF16)
        y3m_s[2:4] = (total[2:4] + y2m_r[...].astype(F32)).astype(BF16)
        hop["y3m"] = send(y3m_s, y3m_r, YM)

    def x_far():
        x2p_s[...] = row_part[xx(2), 0].astype(BF16)
        x2m_s[...] = row_part[xx(2), 1].astype(BF16)
        hop["x2p"] = send(x2p_s, x2p_r, XP)
        hop["x2m"] = send(x2m_s, x2m_r, XM)

    def x_up():
        hop["x2p"].wait_recv()
        x3p_s[0] = (row_part[xx(1), 0] + x2p_r[...].astype(F32)).astype(BF16)
        x3p_s[1] = row_part[xx(1), 1].astype(BF16)
        hop["x3p"] = send(x3p_s, x3p_r, XP)

    def x_down():
        hop["x2m"].wait_recv()
        x3m_s[0] = row_part[xx(3), 0].astype(BF16)
        x3m_s[1] = (row_part[xx(3), 1] + x2m_r[...].astype(F32)).astype(BF16)
        hop["x3m"] = send(x3m_s, x3m_r, XM)

    tiles = [(s, i) for s in range(NY) for i in range(NX)]
    total_tiles = len(tiles)
    for t in range(total_tiles + 2):
        if t < total_tiles:
            score(*tiles[t])
        if 1 <= t <= total_tiles:
            elem(*tiles[t - 1])
        if t >= 2:
            s, i = tiles[t - 2]
            row_grad(s, i)
            if i == NX - 1:
                ex[s] = col_grad(s)
            if (s, i) == (2, 0):
                y_far()
            if (s, i) == (3, 0):
                x_far()
                y_up()
            if (s, i) == (3, 2):
                y_down()
            if (s, i) == (3, 3):
                x_up()
                x_down()

    ex[3].wait_recv()
    hop["y3p"].wait_recv()
    hop["y3m"].wait_recv()
    q_sum[...] = (col_part[3] + ex_r[3].astype(F32)) + (
        y3p_r[...].astype(F32) + y3m_r[...].astype(F32)
    )
    z2p_s[...] = q_sum[zz(2), 0:32].astype(BF16)
    z2m_s[...] = q_sum[zz(2), 32:64].astype(BF16)
    z2p, z2m = send(z2p_s, z2p_r, ZP), send(z2m_s, z2m_r, ZM)
    hop["x3p"].wait_recv()
    hop["x3m"].wait_recv()
    w_s[...] = (
        row_part[x, 1 - zl] + (x3p_r[1 - zl].astype(F32) + x3m_r[1 - zl].astype(F32))
    ).astype(BF16)
    w = send(w_s, w_r, LO)
    z2p.wait_recv()
    z3p_s[0:32] = (q_sum[zz(1), 0:32] + z2p_r[...].astype(F32)).astype(BF16)
    z3p_s[32:64] = q_sum[zz(1), 32:64].astype(BF16)
    z3p = send(z3p_s, z3p_r, ZP)
    z2m.wait_recv()
    z3m_s[0:32] = q_sum[zz(3), 0:32].astype(BF16)
    z3m_s[32:64] = (q_sum[zz(3), 32:64] + z2m_r[...].astype(F32)).astype(BF16)
    z3m = send(z3m_s, z3m_r, ZM)
    for cp in l_acc:
        cp.wait()

    def update(emb, acc, grad, new_ref, acc_ref):
        acc_new = acc + grad * grad
        acc_ref[...] = acc_new
        new_ref[...] = emb - LEARN_RATE * grad / jnp.sqrt(acc_new)

    own = row_part[x, zl] + (x3p_r[zl].astype(F32) + x3m_r[zl].astype(F32))
    w.wait_recv()
    update(remb[...], racc[...], (own + w_r[...].astype(F32)) * (1 / 256), rnew_ref, raccn_ref)
    z3p.wait_recv()
    z3m.wait_recv()
    total = q_sum[zh] + (z3p_r[...].astype(F32) + z3m_r[...].astype(F32))
    update(cemb[...], cacc[...], total * (1 / 128), cnew_ref, caccn_ref)
    for cp in copies:
        cp.wait_send()


def local(counts, row_ids, col_ids, row_marginal, col_marginal, row_emb, row_acc, col_emb, col_acc):
    any_spec = pl.BlockSpec(memory_space=pl.ANY)
    vmem = pltpu.VMEM
    i32 = jnp.int32
    scratch = [
        vmem((ROWS, COLS), i32), vmem((1, ROWS), i32), vmem((1, COLS), i32),
        vmem((320, 128), i32), vmem((128, 128), i32),
        vmem((RB, K), F32), vmem((RB, K), F32), vmem((CB, K), F32), vmem((CB, K), F32),
        vmem((NX, NZL, RB, K), BF16), vmem((K, ROWS), BF16),
        vmem((NY, NZH, NC, CB, K), BF16), vmem((NY, K, QB), BF16),
        vmem((ROWS, 128), F32), vmem((SUB, COLS), F32),
        vmem((2, XB, QB), F32), vmem((2, ROWS, QB), BF16),
        vmem((NX, NZL, RB, K), F32), vmem((2, NZH, NC, CB, K), F32),
        vmem((NY, NZH, CB, K), F32), vmem((NZH, CB, K), F32),
    ]
    scratch += [vmem((NY, NZH, CB, K), BF16)] * 2
    scratch += [vmem((2, CB, K), BF16)] * 4
    scratch += [vmem((4, CB, K), BF16)] * 4
    scratch += [vmem((32, K), BF16)] * 4
    scratch += [vmem((CB, K), BF16)] * 4
    scratch += [vmem((RB, K), BF16)] * 4
    scratch += [vmem((NZL, RB, K), BF16)] * 4
    scratch += [vmem((RB, K), BF16)] * 2
    scratch += [
        pltpu.SemaphoreType.DMA((12,)),
        pltpu.SemaphoreType.DMA((N_SEMS,)),
        pltpu.SemaphoreType.DMA((N_SEMS,)),
    ]
    row_out = jax.ShapeDtypeStruct((RB, K), F32)
    col_out = jax.ShapeDtypeStruct((CB, K), F32)
    return pl.pallas_call(
        kernel,
        out_shape=(row_out, row_out, col_out, col_out),
        in_specs=[any_spec] * 9,
        out_specs=(pl.BlockSpec(memory_space=pltpu.VMEM),) * 4,
        scratch_shapes=scratch,
        compiler_params=pltpu.CompilerParams(
            collective_id=0, has_side_effects=True, vmem_limit_bytes=48 * 1024 * 1024
        ),
        name="step",
    )(
        counts,
        row_ids.reshape(1, ROWS),
        col_ids.reshape(1, COLS),
        row_marginal.reshape(320, 128),
        col_marginal.reshape(128, 128),
        row_emb, row_acc, col_emb, col_acc,
    )


def solution(mesh):
    placed = (
        P("gr", "gc"),
        P("gr"),
        P("gc"),
        P(),
        P(),
        P(("gr", "gc"), None),
        P(("gr", "gc"), None),
        P(("gc", "gr"), None),
        P(("gc", "gr"), None),
    )
    return jax.shard_map(
        local,
        mesh=mesh,
        in_specs=placed,
        out_specs=(
            P(("gr", "gc"), None),
            P(("gr", "gc"), None),
            P(("gc", "gr"), None),
            P(("gc", "gr"), None),
        ),
        check_vma=False,
    )
```

```python
import functools

import jax
import jax.numpy as jnp
from jax import lax
from jax.experimental import pallas as pl
from jax.experimental.pallas import tpu as pltpu
from jax.sharding import PartitionSpec as P

F32 = jnp.float32
BF16 = jnp.bfloat16
MESH = pl.DeviceIdType.MESH

LEARN_RATE = 0.5
K = 256
NX, NZL = 4, 2
NZH, NY, NC = 4, 4, 2
RB = 160
CB = 64
XB = RB * NZL
QB = NZH * NC * CB
ROWS = NX * XB
COLS = NY * QB
SUB = 16
TILES = (
    (1, 0), (3, 0), (0, 1), (1, 1), (3, 1), (0, 3), (1, 3), (3, 3),
    (2, 1), (2, 3), (2, 2), (2, 0), (1, 2), (3, 2), (0, 2), (0, 0),
)
N_SEMS = 64


def lookup(table, ids):
    high = lax.shift_right_logical(ids, 7)
    low = ids & 127
    n_high, n = table.shape[0], ids.shape[1]
    hot = (lax.broadcasted_iota(jnp.int32, (n_high, n), 0) == high).astype(F32).astype(BF16)
    digits = [
        lax.shift_right_logical(table, 16),
        lax.shift_right_logical(table, 8) & 255,
        table & 255,
    ]
    parts = [
        jnp.dot(d.astype(F32).T.astype(BF16), hot, preferred_element_type=F32) for d in digits
    ]
    whole = parts[0] * 65536.0 + parts[1] * 256.0 + parts[2]
    mine = lax.broadcasted_iota(jnp.int32, (128, n), 0) == low
    return jnp.log(jnp.sum(jnp.where(mine, whole, 0.0), axis=0, keepdims=True))


def kernel(
    cnt_hbm, rid_hbm, cid_hbm, rmar_hbm, cmar_hbm, remb_hbm, racc_hbm, cemb_hbm, cacc_hbm,
    rnew_ref, raccn_ref, cnew_ref, caccn_ref,
    cnt, rid, cid, rmar, cmar, remb, racc, cemb, cacc,
    rows, rows_t, cols, cols_t, row_term, col_term,
    s_ref, g_ref, row_part, col_tmp, col_part,
    ex_s, ex_r, col_s, y_r, z_r, far_s, far_r, row_s, row_r, w_s, w_r,
    local_sem, send_sem, recv_sem,
):
    gr = lax.axis_index("gr")
    gc = lax.axis_index("gc")
    c = lax.rem(gr, NC)
    y = lax.rem(gr // NC, NY)
    zh = gr // (NC * NY)
    zl = lax.rem(gc, NZL)
    x = gc // NZL

    def at(dx=0, dzl=0, dzh=0, dy=0, dc=0):
        g = (lax.rem(zh + dzh, NZH) * NY + lax.rem(y + dy, NY)) * NC + lax.rem(c + dc, NC)
        k = lax.rem(x + dx, NX) * NZL + lax.rem(zl + dzl, NZL)
        return (g, k)

    XP, XM, CO, LO = at(dx=1), at(dx=3), at(dc=1), at(dzl=1)
    neighbours = [at(dzh=j) for j in (2, 1, 3)] + [at(dy=d) for d in (2, 1, 3)]
    neighbours += [at(dx=2), XP, XM, LO, CO]

    loads = []

    def load(src, dst):
        cp = pltpu.make_async_copy(src, dst, local_sem.at[len(loads)])
        cp.start()
        loads.append(cp)
        return cp

    l_remb, l_cemb = load(remb_hbm, remb), load(cemb_hbm, cemb)
    barrier = pltpu.get_barrier_semaphore()
    for n in neighbours:
        pl.semaphore_signal(barrier, inc=1, device_id=n, device_id_type=MESH)
    l_ids = [load(rid_hbm, rid), load(cid_hbm, cid), load(rmar_hbm, rmar), load(cmar_hbm, cmar)]
    l_cnt = [
        load(cnt_hbm.at[pl.ds(i * XB, XB)], cnt.at[pl.ds(i * XB, XB)]) for i in range(NX)
    ]
    l_acc = [load(racc_hbm, racc), load(cacc_hbm, cacc)]

    copies = []

    def send(src, dst, target):
        i = len(copies)
        cp = pltpu.make_async_remote_copy(
            src_ref=src, dst_ref=dst, send_sem=send_sem.at[i], recv_sem=recv_sem.at[i],
            device_id=target, device_id_type=MESH,
        )
        cp.start()
        copies.append(cp)
        return cp

    def zz(d):
        return lax.rem(zh + d, NZH)

    def yy(d):
        return lax.rem(y + d, NY)

    def xx(d):
        return lax.rem(x + d, NX)

    def same(ref, target):
        return send(ref, ref, target)

    l_remb.wait()
    rows[x, zl] = (remb[...] * 0.5).astype(BF16)
    l_cemb.wait()
    cols[y, zh, c] = cemb[...].astype(BF16)
    pl.semaphore_wait(barrier, len(neighbours))

    own_r, own_c = rows.at[x, zl], cols.at[y, zh, c]
    z_in, y_in, core_in, q_in = {}, {}, {}, {}

    def spread(j):
        piece = cols.at[y, zz(NZH - j), c]
        core_in[j] = same(piece, CO)
        for d in (1, 3):
            y_in[j, d] = same(piece, at(dy=d))

    for j in (1, 3, 2):
        z_in[j] = same(own_c, at(dzh=j))
    r_lo = same(own_r, LO)
    r_p0, r_m0 = same(own_r, XP), same(own_r, XM)
    spread(0)

    for cp in l_ids:
        cp.wait()
    col_log = lookup(cmar[...], cid[...])
    col_term[...] = jnp.broadcast_to(0.5 * col_log, col_term.shape)
    r_lo.wait_recv()
    other_r = rows.at[x, 1 - zl]
    r_p1, r_m1 = same(other_r, XP), same(other_r, XM)
    for j in (1, 3):
        z_in[j].wait_recv()
        spread(j)
    r_p0.wait_recv()
    r_fp = same(rows.at[xx(3), zl, pl.ds(0, RB // 2)], XP)
    r_m0.wait_recv()
    r_fm = same(rows.at[xx(1), zl, pl.ds(RB // 2, RB // 2)], XM)
    z_in[2].wait_recv()
    spread(2)
    for j in range(NZH):
        y_in[j, 2] = same(cols.at[y, zz(NZH - j), c], at(dy=2))
    row_log = lookup(rmar[...], rid[...].reshape(1, ROWS))
    log_total = jnp.log(jnp.sum(rmar[...].astype(F32)))
    row_vec = 0.5 * (row_log - log_total)
    for b in range(ROWS // 128):
        piece = jnp.broadcast_to(row_vec[:, b * 128 : (b + 1) * 128], (128, 128))
        row_term[b * 128 : (b + 1) * 128, :] = piece.T
    rest = {}

    def rows_ready(dx):
        rows_t[:, dx * XB : (dx + 1) * XB] = rows[xx(dx)].reshape(XB, K).T

    def cols_ready(e):
        cols_t[e] = cols[yy(e)].reshape(QB, K).T

    def cols_to_core(e):
        for j in range(NZH):
            y_in[j, NY - e].wait_recv()
        q_in[e] = same(cols.at[yy(e), :, c], CO)

    def before(t):
        if t == 0:
            rows_ready(0)
            for j in range(NZH):
                core_in[j].wait_recv()
            cols_ready(0)
            r_m1.wait_recv()
            rows_ready(1)
            for cp in l_cnt:
                cp.wait()
        if t == 1:
            r_p1.wait_recv()
            rows_ready(3)
            r_fp.wait_recv()
            r_fm.wait_recv()
            rest["r_lo2"] = same(rows.at[xx(2), zl], LO)
        if t == 2:
            cols_to_core(1)
            cols_to_core(3)
            q_in[1].wait_recv()
            cols_ready(1)
        if t == 4:
            cols_to_core(2)
        if t == 5:
            q_in[3].wait_recv()
            cols_ready(3)
        if t == 8:
            rest["r_lo2"].wait_recv()
            rows_ready(2)
        if t == 10:
            q_in[2].wait_recv()
            cols_ready(2)

    def score(t):
        dx, e = TILES[t]
        s_ref[t % 2] = jnp.dot(
            rows[xx(dx)].reshape(XB, K), cols_t[e], preferred_element_type=F32
        )

    def elem(t):
        dx, e = TILES[t]
        r_at = pl.multiple_of(xx(dx) * XB, XB)
        for z in range(NZH):
            c_at = pl.multiple_of(z * QB + yy(e) * 128, 128)
            c_row = col_term[:, pl.ds(c_at, 128)]
            for u in range(XB // SUB):
                at_u = pl.ds(pl.multiple_of(r_at + u * SUB, SUB), SUB)
                n = cnt[at_u, pl.ds(c_at, 128)]
                m = jnp.maximum(n, 1).astype(F32)
                inv = lax.rsqrt(m)
                half = (
                    s_ref[t % 2, u * SUB : (u + 1) * SUB, z * 128 : (z + 1) * 128] + jnp.log(inv)
                ) + (row_term[at_u, :] + c_row)
                g = jnp.where(n > 0, (m * inv + 0.4) * half, jnp.tanh(half) + 1.0)
                at_g = dx * XB + u * SUB
                g_ref[e, at_g : at_g + SUB, z * 128 : (z + 1) * 128] = g.astype(BF16)

    def row_grad(t):
        dx, e = TILES[t]
        part = jnp.dot(
            g_ref[e, dx * XB : (dx + 1) * XB, :],
            cols[yy(e)].reshape(QB, K),
            preferred_element_type=F32,
        ).reshape(NZL, RB, K)
        if dx not in [a for a, _ in TILES[:t]]:
            row_part[dx] = part
        else:
            row_part[dx] += part

    ex, row_in = {}, {}

    def col_grad(e):
        t = jnp.dot(rows_t[...], g_ref[e], preferred_element_type=F32)
        col_tmp[e] = t.T.reshape(NZH, NC, CB, K)
        ex_s[e] = col_tmp[e, :, 1 - c].astype(BF16)
        ex[e] = send(ex_s.at[e], ex_r.at[e], CO)

    y_back, z_back = {}, {}

    def col_out(e):
        ex[e].wait_recv()
        total = col_tmp[e, :, c] + ex_r[e].astype(F32)
        if e == 0:
            for d in (1, 3):
                y_back[d].wait_recv()
                total = total + y_r[d // 2].astype(F32)
        col_s[e] = total.astype(BF16)
        if e % 2:
            y_back[e] = send(col_s.at[e], y_r.at[e // 2], at(dy=e))
        else:
            col_part[e // 2] = total
            for j in (2, 1, 3):
                z_back[e, j] = send(col_s.at[e, zz(j)], z_r.at[e // 2, j - 1], at(dzh=j))

    def z_sum(e):
        for j in (1, 3, 2):
            z_back[e, j].wait_recv()
        total = col_part[e // 2, zh]
        for j in range(NZH - 1):
            total = total + z_r[e // 2, j].astype(F32)
        return total

    def row_out(dx):
        row_s[dx - 1] = row_part[dx].astype(BF16)
        row_in[dx] = send(row_s.at[dx - 1], row_r.at[dx - 1], at(dx=dx))

    n_tiles = len(TILES)
    for t in range(n_tiles + 2):
        late = t == 2
        if t < n_tiles and not late:
            before(t)
            score(t)
        if 1 <= t <= n_tiles:
            elem(t - 1)
        if t >= 2:
            row_grad(t - 2)
        if late:
            before(t)
            score(t)
        if t == 10:
            col_grad(1)
        if t == 11:
            col_grad(3)
        if t == 13:
            col_out(1)
            row_out(2)
        if t == 14:
            row_out(1)
            col_out(3)
        if t == 15:
            row_out(3)
        if t == 16:
            col_grad(2)
        if t == 17:
            col_grad(0)

    col_out(2)
    col_out(0)
    for dx in (2, 1, 3):
        row_in[dx].wait_recv()

    def row_sum(at_zl):
        total = row_part[0, at_zl]
        for i in range(NX - 1):
            total = total + row_r[i, at_zl].astype(F32)
        return total

    w_s[...] = row_sum(1 - zl).astype(BF16)
    w = send(w_s, w_r, LO)
    far_s[...] = z_sum(2).astype(BF16)
    far = send(far_s, far_r, at(dy=2))
    own = row_sum(zl)
    for cp in l_acc:
        cp.wait()

    def update(emb, acc, grad, new_ref, acc_ref):
        acc_new = acc + grad * grad
        acc_ref[...] = acc_new
        new_ref[...] = emb - LEARN_RATE * grad / jnp.sqrt(acc_new)

    w.wait_recv()
    update(remb[...], racc[...], (own + w_r[...].astype(F32)) * (1 / 256), rnew_ref, raccn_ref)
    total = z_sum(0)
    far.wait_recv()
    total = total + far_r[...].astype(F32)
    update(cemb[...], cacc[...], total * (1 / 128), cnew_ref, caccn_ref)
    for cp in copies:
        cp.wait_send()


def hand_over(*refs):
    n = len(refs) // 2
    sem = refs[-1]
    moves = [pltpu.make_async_copy(refs[i], refs[n + i], sem.at[i]) for i in range(n)]
    for m in moves:
        m.start()
    for m in moves:
        m.wait()


def local(counts, row_ids, col_ids, row_marginal, col_marginal, row_emb, row_acc, col_emb, col_acc):
    hbm = pl.BlockSpec(memory_space=pltpu.HBM)
    vmem = pltpu.VMEM
    i32 = jnp.int32
    scratch = [
        vmem((ROWS, COLS), i32), vmem((ROWS,), i32), vmem((1, COLS), i32),
        vmem((320, 128), i32), vmem((128, 128), i32),
        vmem((RB, K), F32), vmem((RB, K), F32), vmem((CB, K), F32), vmem((CB, K), F32),
        vmem((NX, NZL, RB, K), BF16), vmem((K, ROWS), BF16),
        vmem((NY, NZH, NC, CB, K), BF16), vmem((NY, K, QB), BF16),
        vmem((ROWS, 128), F32), vmem((SUB, COLS), F32),
        vmem((2, XB, QB), F32), vmem((NY, ROWS, QB), BF16),
        vmem((NX, NZL, RB, K), F32), vmem((NY, NZH, NC, CB, K), F32), vmem((2, NZH, CB, K), F32),
        vmem((NY, NZH, CB, K), BF16), vmem((NY, NZH, CB, K), BF16), vmem((NY, NZH, CB, K), BF16),
        vmem((2, NZH, CB, K), BF16), vmem((2, NZH - 1, CB, K), BF16),
        vmem((CB, K), BF16), vmem((CB, K), BF16),
        vmem((NX - 1, NZL, RB, K), BF16), vmem((NX - 1, NZL, RB, K), BF16),
        vmem((RB, K), BF16), vmem((RB, K), BF16),
        pltpu.SemaphoreType.DMA((12,)),
        pltpu.SemaphoreType.DMA((N_SEMS,)),
        pltpu.SemaphoreType.DMA((N_SEMS,)),
    ]
    shapes = ((RB, K), (RB, K), (CB, K), (CB, K))
    operands = (
        counts, row_ids, col_ids.reshape(1, COLS),
        row_marginal.reshape(320, 128), col_marginal.reshape(128, 128),
        row_emb, row_acc, col_emb, col_acc,
    )
    out = pl.pallas_call(
        kernel,
        out_shape=tuple(pltpu.VMEM(s, F32) for s in shapes),
        in_specs=[hbm] * 9,
        out_specs=(pl.BlockSpec(memory_space=pltpu.VMEM),) * 4,
        scratch_shapes=scratch,
        compiler_params=pltpu.CompilerParams(
            collective_id=0, has_side_effects=True, vmem_limit_bytes=48 * 1024 * 1024
        ),
        name="step",
    )(*[pltpu.with_memory_space_constraint(a, pltpu.HBM) for a in operands])
    return pl.pallas_call(
        hand_over,
        out_shape=tuple(jax.ShapeDtypeStruct(s, F32) for s in shapes),
        in_specs=[pl.BlockSpec(memory_space=pltpu.VMEM)] * 4,
        out_specs=(hbm,) * 4,
        scratch_shapes=[pltpu.SemaphoreType.DMA((4,))],
        name="hand_over",
    )(*[pltpu.with_memory_space_constraint(a, pltpu.VMEM) for a in out])


def solution(mesh):
    placed = (
        P("gr", "gc"),
        P("gr"),
        P("gc"),
        P(),
        P(),
        P(("gr", "gc"), None),
        P(("gr", "gc"), None),
        P(("gc", "gr"), None),
        P(("gc", "gr"), None),
    )
    return jax.shard_map(
        local,
        mesh=mesh,
        in_specs=placed,
        out_specs=(
            P(("gr", "gc"), None),
            P(("gr", "gc"), None),
            P(("gc", "gr"), None),
            P(("gc", "gr"), None),
        ),
        check_vma=False,
    )
```

```python
import functools

import jax
import jax.numpy as jnp
from jax import lax
from jax.experimental import pallas as pl
from jax.experimental.pallas import tpu as pltpu
from jax.sharding import PartitionSpec as P

F32 = jnp.float32
BF16 = jnp.bfloat16
MESH = pl.DeviceIdType.MESH

LEARN_RATE = 0.5
K = 256
NX, NZL = 4, 2
NZH, NY, NC = 4, 4, 2
RB = 160
CB = 64
XB = RB * NZL
QB = NY * NC * CB
ROWS = NX * XB
COLS = NZH * QB
SUB = 16
TILES = (
    (0, 0), (3, 0), (1, 0), (2, 0), (0, 1), (3, 1), (1, 1), (2, 1),
    (0, 2), (3, 2), (1, 2), (2, 2), (2, 3), (1, 3), (3, 3), (0, 3),
)
LATE = (1, 3, 4, 8, 12)
SPREAD = {1: 2, 2: 3}
FORWARD = {3: (1,), 6: (2,), 9: (3,)}
PIECES = (2, 1, 3, 0)
N_SEMS = 80


def lookup(table, ids):
    high = lax.shift_right_logical(ids, 7)
    low = ids & 127
    n_high, n = table.shape[0], ids.shape[1]
    hot = (lax.broadcasted_iota(jnp.int32, (n_high, n), 0) == high).astype(F32).astype(BF16)
    digits = [
        lax.shift_right_logical(table, 16),
        lax.shift_right_logical(table, 8) & 255,
        table & 255,
    ]
    parts = [
        jnp.dot(d.astype(F32).T.astype(BF16), hot, preferred_element_type=F32) for d in digits
    ]
    whole = parts[0] * 65536.0 + parts[1] * 256.0 + parts[2]
    mine = lax.broadcasted_iota(jnp.int32, (128, n), 0) == low
    return jnp.log(jnp.sum(jnp.where(mine, whole, 0.0), axis=0, keepdims=True))


def kernel(
    cnt_hbm, rid_hbm, cid_hbm, rmar_hbm, cmar_hbm, remb_hbm, racc_hbm, cemb_hbm, cacc_hbm,
    rnew_ref, raccn_ref, cnew_ref, caccn_ref,
    cnt, rid, cid, rmar, cmar, remb, racc, cemb, cacc,
    rows, rows_t, cols, row_term, col_term,
    s_ref, g_ref, row_part, col_tmp, col_part,
    ex_s, ex_r, col_s, y_r, z_s, z_r, row_s, row_r, w_s, w_r,
    local_sem, send_sem, recv_sem, z_send, z_recv, sum_send, sum_recv, here,
):
    gr = lax.axis_index("gr")
    gc = lax.axis_index("gc")
    c = lax.rem(gr, NC)
    y = lax.rem(gr // NC, NY)
    zh = gr // (NC * NY)
    zl = lax.rem(gc, NZL)
    x = gc // NZL

    def at(dx=0, dzl=0, dzh=0, dy=0, dc=0):
        g = (lax.rem(zh + dzh, NZH) * NY + lax.rem(y + dy, NY)) * NC + lax.rem(c + dc, NC)
        k = lax.rem(x + dx, NX) * NZL + lax.rem(zl + dzl, NZL)
        return (g, k)

    XP, XM, CO, LO = at(dx=1), at(dx=3), at(dc=1), at(dzl=1)
    neighbours = [at(dy=d) for d in (2, 1, 3)] + [at(dx=2), XP, XM, LO, CO]

    def z_device(to):
        return ((to * NY + y) * NC + c, gc)

    place = [zh] + [jnp.where(zh <= i, i + 1, i) for i in range(NZH - 1)]

    loads = []

    def load(src, dst):
        cp = pltpu.make_async_copy(src, dst, local_sem.at[len(loads)])
        cp.start()
        loads.append(cp)
        return cp

    l_remb, l_cemb = load(remb_hbm, remb), load(cemb_hbm, cemb)
    barrier = pltpu.get_barrier_semaphore()
    for n in neighbours:
        pl.semaphore_signal(barrier, inc=1, device_id=n, device_id_type=MESH)
    for to in range(1, NZH):

        @pl.when(zh < to)
        def _(to=to):
            pl.semaphore_signal(barrier, inc=1, device_id=z_device(to), device_id_type=MESH)

    l_ids = [load(rid_hbm, rid), load(cid_hbm, cid), load(rmar_hbm, rmar), load(cmar_hbm, cmar)]
    l_cnt = [
        load(cnt_hbm.at[pl.ds(i * XB, XB)], cnt.at[pl.ds(i * XB, XB)]) for i in range(NX)
    ]
    l_acc = [load(racc_hbm, racc), load(cacc_hbm, cacc)]

    copies = []

    def send(src, dst, target):
        i = len(copies)
        cp = pltpu.make_async_remote_copy(
            src_ref=src, dst_ref=dst, send_sem=send_sem.at[i], recv_sem=recv_sem.at[i],
            device_id=target, device_id_type=MESH,
        )
        cp.start()
        copies.append(cp)
        return cp

    def yy(d):
        return lax.rem(y + d, NY)

    def xx(d):
        return lax.rem(x + d, NX)

    def same(ref, target):
        return send(ref, ref, target)

    l_remb.wait()
    rows[x, zl] = (remb[...] * 0.5).astype(BF16)
    l_cemb.wait()
    cols[zh, y, c] = cemb[...].astype(BF16)
    pl.semaphore_wait(barrier, len(neighbours) + zh)

    own_r, own_c = rows.at[x, zl], cols.at[zh, y, c]
    y_in, core_in = {}, {}

    def z_copy(to):
        return pltpu.make_async_remote_copy(
            src_ref=own_c, dst_ref=own_c, send_sem=z_send.at[to], recv_sem=z_recv.at[zh],
            device_id=z_device(to), device_id_type=MESH,
        )

    for to in range(NZH - 1):

        @pl.when(zh > to)
        def _(to=to):
            pl.semaphore_signal(
                here.at[zh], inc=1, device_id=z_device(to), device_id_type=MESH
            )
            z_copy(to).start()

    def spread(b):
        piece = cols.at[place[b], y, c]
        if b:
            pltpu.make_async_remote_copy(
                src_ref=piece, dst_ref=piece, send_sem=z_send.at[place[b]],
                recv_sem=z_recv.at[place[b]], device_id=z_device(place[b]), device_id_type=MESH,
            ).wait_recv()
        core_in[b, 0] = same(piece, CO)
        for d in (1, 3, 2):
            y_in[b, d] = same(piece, at(dy=d))

    def cols_to_core(b):
        for d in (1, 3, 2):
            y_in[b, d].wait_recv()
            core_in[b, d] = same(cols.at[place[b], yy(NY - d), c], CO)

    spread(0)
    r_lo = same(own_r, LO)
    r_p0, r_m0, r_x2 = same(own_r, XP), same(own_r, XM), same(own_r, at(dx=2))

    for cp in l_ids:
        cp.wait()
    col_log = lookup(cmar[...], cid[...])
    col_term[...] = jnp.broadcast_to(0.5 * col_log, col_term.shape)
    r_lo.wait_recv()
    other_r = rows.at[x, 1 - zl]
    r_p1, r_m1 = same(other_r, XP), same(other_r, XM)
    for to in range(1, NZH):

        @pl.when(zh < to)
        def _(to=to):
            pl.semaphore_wait(here.at[to], 1)
            z_copy(to).start()

    spread(1)
    r_x2.wait_recv()
    r_lo2 = same(rows.at[xx(2), zl], LO)
    cols_to_core(0)
    row_log = lookup(rmar[...], rid[...].reshape(1, ROWS))
    log_total = jnp.log(jnp.sum(rmar[...].astype(F32)))
    row_vec = 0.5 * (row_log - log_total)
    for b in range(ROWS // 128):
        piece = jnp.broadcast_to(row_vec[:, b * 128 : (b + 1) * 128], (128, 128))
        row_term[b * 128 : (b + 1) * 128, :] = piece.T
    def rows_ready(dx):
        rows_t[:, dx * XB : (dx + 1) * XB] = rows[xx(dx)].reshape(XB, K).T

    def cols_ready(b):
        for d in range(NY):
            core_in[b, d].wait_recv()

    def before(t):
        dx, e = TILES[t]
        if t in SPREAD:
            spread(SPREAD[t])
        for b in FORWARD.get(t, ()):
            cols_to_core(b)
        if dx not in [a for a, _ in TILES[:t]]:
            for cp in {0: (), 1: (r_m0, r_m1), 2: (r_lo2,), 3: (r_p0, r_p1)}[dx]:
                cp.wait_recv()
            rows_ready(dx)
        if e not in [a for _, a in TILES[:t]]:
            cols_ready(e)
        if t == 0:
            for cp in l_cnt:
                cp.wait()

    def score(t):
        dx, e = TILES[t]
        s_ref[t % 2] = jnp.dot(
            rows[xx(dx)].reshape(XB, K), cols[place[e]].reshape(QB, K).T, preferred_element_type=F32
        )

    def elem(t):
        dx, e = TILES[t]
        r_at = pl.multiple_of(xx(dx) * XB, XB)
        for z in range(QB // 128):
            c_at = pl.multiple_of(place[e] * QB + z * 128, 128)
            c_row = col_term[:, pl.ds(c_at, 128)]
            for u in range(XB // SUB):
                at_u = pl.ds(pl.multiple_of(r_at + u * SUB, SUB), SUB)
                n = cnt[at_u, pl.ds(c_at, 128)]
                m = jnp.maximum(n, 1).astype(F32)
                inv = lax.rsqrt(m)
                half = (
                    s_ref[t % 2, u * SUB : (u + 1) * SUB, z * 128 : (z + 1) * 128] + jnp.log(inv)
                ) + (row_term[at_u, :] + c_row)
                g = jnp.where(n > 0, (m * inv + 0.4) * half, jnp.tanh(half) + 1.0)
                at_g = dx * XB + u * SUB
                g_ref[e, at_g : at_g + SUB, z * 128 : (z + 1) * 128] = g.astype(BF16)

    def row_grad(t):
        dx, e = TILES[t]
        part = jnp.dot(
            g_ref[e, dx * XB : (dx + 1) * XB, :],
            cols[place[e]].reshape(QB, K),
            preferred_element_type=F32,
        ).reshape(NZL, RB, K)
        if dx not in [a for a, _ in TILES[:t]]:
            row_part[dx] = part
        else:
            row_part[dx] += part

    ex, row_in = {}, {}

    def col_grad(e):
        t = jnp.dot(rows_t[...], g_ref[e], preferred_element_type=F32)
        col_tmp[e] = t.T.reshape(NY, NC, CB, K)
        for d in PIECES:
            ex_s[e, yy(d)] = col_tmp[e, yy(d), 1 - c].astype(BF16)
            ex[e, d] = send(ex_s.at[e, yy(d)], ex_r.at[e, yy(d)], CO)

    y_back, z_back = {}, {}

    def both_cores(e, d):
        ex[e, d].wait_recv()
        return col_tmp[e, yy(d), c] + ex_r[e, yy(d)].astype(F32)

    def col_out(e):
        for d in PIECES:
            if d:
                col_s[e, d - 1] = both_cores(e, d).astype(BF16)
                y_back[e, d] = send(col_s.at[e, d - 1], y_r.at[e, d - 1], at(dy=d))
            else:
                col_part[e] = both_cores(e, d)

    def sum_copy(e):
        return pltpu.make_async_remote_copy(
            src_ref=z_s.at[e - 1], dst_ref=z_r.at[zh], send_sem=sum_send.at[e],
            recv_sem=sum_recv.at[zh], device_id=z_device(place[e]), device_id_type=MESH,
        )

    def sum_in(e):
        pltpu.make_async_remote_copy(
            src_ref=z_s.at[e - 1], dst_ref=z_r.at[place[e]], send_sem=sum_send.at[e],
            recv_sem=sum_recv.at[place[e]], device_id=z_device(place[e]), device_id_type=MESH,
        ).wait_recv()

    def col_sum(e):
        total = col_part[e]
        for d in (1, 3, 2):
            y_back[e, d].wait_recv()
            total = total + y_r[e, d - 1].astype(F32)
        if e:
            z_s[e - 1] = total.astype(BF16)
            z_back[e] = sum_copy(e)
            z_back[e].start()
        else:
            col_part[0] = total

    def row_out(dx):
        for p in (1, 0):
            at_zl = lax.rem(zl + p, NZL)
            row_s[dx - 1, at_zl] = row_part[dx, at_zl].astype(BF16)
            row_in[dx, p] = send(row_s.at[dx - 1, at_zl], row_r.at[dx - 1, at_zl], at(dx=dx))

    n_tiles = len(TILES)
    row_end = {dx: max(i for i in range(n_tiles) if TILES[i][0] == dx) for dx in range(NX)}
    col_end = {e: max(i for i in range(n_tiles) if TILES[i][1] == e) for e in range(NZH)}
    col_order = sorted(range(NZH), key=col_end.get)
    for t in range(n_tiles + 2):
        late = t in LATE
        if t < n_tiles and not late:
            before(t)
            score(t)
        if 1 <= t <= n_tiles:
            elem(t - 1)
        if t >= 2:
            row_grad(t - 2)
        if late:
            before(t)
            score(t)
        for dx in range(1, NX):
            if t == row_end[dx] + 2:
                row_out(dx)
        for e in range(NZH):
            if t == col_end[e] + 2:
                col_grad(e)
        for e in col_order:
            if t == col_end[e] + 4:
                col_out(e)
            if t == col_end[e] + 10:
                col_sum(e)

    for e in col_order:
        if col_end[e] + 4 >= n_tiles + 2:
            col_out(e)
    left = [e for e in col_order if col_end[e] + 10 >= n_tiles + 2]
    for e in left[:-1]:
        col_sum(e)

    def row_sum(at_zl):
        total = row_part[0, at_zl]
        for i in range(NX - 1):
            total = total + row_r[i, at_zl].astype(F32)
        return total

    for dx in sorted((1, 2, 3), key=row_end.get):
        row_in[dx, 1].wait_recv()
    w_s[...] = row_sum(1 - zl).astype(BF16)
    w = send(w_s, w_r, LO)
    for e in left[-1:]:
        col_sum(e)
    for dx in (1, 3, 2):
        row_in[dx, 0].wait_recv()
    own = row_sum(zl)
    for cp in l_acc:
        cp.wait()

    def update(emb, acc, grad, new_ref, acc_ref):
        acc_new = acc + grad * grad
        acc_ref[...] = acc_new
        new_ref[...] = emb - LEARN_RATE * grad / jnp.sqrt(acc_new)

    w.wait_recv()
    update(remb[...], racc[...], (own + w_r[...].astype(F32)) * (1 / 256), rnew_ref, raccn_ref)
    total = col_part[0]
    for e in (1, 2, 3):
        sum_in(e)
        total = total + z_r[place[e]].astype(F32)
    update(cemb[...], cacc[...], total * (1 / 128), cnew_ref, caccn_ref)
    for cp in copies:
        cp.wait_send()
    for e in range(1, NZH):
        z_back[e].wait_send()
        z_copy(place[e]).wait_send()


def hand_over(*refs):
    n = len(refs) // 2
    sem = refs[-1]
    moves = [pltpu.make_async_copy(refs[i], refs[n + i], sem.at[i]) for i in range(n)]
    for m in moves:
        m.start()
    for m in moves:
        m.wait()


def local(counts, row_ids, col_ids, row_marginal, col_marginal, row_emb, row_acc, col_emb, col_acc):
    hbm = pl.BlockSpec(memory_space=pltpu.HBM)
    vmem = pltpu.VMEM
    i32 = jnp.int32
    scratch = [
        vmem((ROWS, COLS), i32), vmem((ROWS,), i32), vmem((1, COLS), i32),
        vmem((320, 128), i32), vmem((128, 128), i32),
        vmem((RB, K), F32), vmem((RB, K), F32), vmem((CB, K), F32), vmem((CB, K), F32),
        vmem((NX, NZL, RB, K), BF16), vmem((K, ROWS), BF16),
        vmem((NZH, NY, NC, CB, K), BF16),
        vmem((ROWS, 128), F32), vmem((SUB, COLS), F32),
        vmem((2, XB, QB), F32), vmem((NZH, ROWS, QB), BF16),
        vmem((NX, NZL, RB, K), F32), vmem((NZH, NY, NC, CB, K), F32), vmem((NZH, CB, K), F32),
        vmem((NZH, NY, CB, K), BF16), vmem((NZH, NY, CB, K), BF16),
        vmem((NZH, NY - 1, CB, K), BF16), vmem((NZH, NY - 1, CB, K), BF16),
        vmem((NZH - 1, CB, K), BF16), vmem((NZH, CB, K), BF16),
        vmem((NX - 1, NZL, RB, K), BF16), vmem((NX - 1, NZL, RB, K), BF16),
        vmem((RB, K), BF16), vmem((RB, K), BF16),
        pltpu.SemaphoreType.DMA((12,)),
        pltpu.SemaphoreType.DMA((N_SEMS,)),
        pltpu.SemaphoreType.DMA((N_SEMS,)),
        pltpu.SemaphoreType.DMA((NZH,)),
        pltpu.SemaphoreType.DMA((NZH,)),
        pltpu.SemaphoreType.DMA((NZH,)),
        pltpu.SemaphoreType.DMA((NZH,)),
        pltpu.SemaphoreType.REGULAR((NZH,)),
    ]
    shapes = ((RB, K), (RB, K), (CB, K), (CB, K))
    operands = (
        counts, row_ids, col_ids.reshape(1, COLS),
        row_marginal.reshape(320, 128), col_marginal.reshape(128, 128),
        row_emb, row_acc, col_emb, col_acc,
    )
    out = pl.pallas_call(
        kernel,
        out_shape=tuple(pltpu.VMEM(s, F32) for s in shapes),
        in_specs=[hbm] * 9,
        out_specs=(pl.BlockSpec(memory_space=pltpu.VMEM),) * 4,
        scratch_shapes=scratch,
        compiler_params=pltpu.CompilerParams(
            collective_id=0, has_side_effects=True, vmem_limit_bytes=48 * 1024 * 1024
        ),
        name="step",
    )(*[pltpu.with_memory_space_constraint(a, pltpu.HBM) for a in operands])
    return pl.pallas_call(
        hand_over,
        out_shape=tuple(jax.ShapeDtypeStruct(s, F32) for s in shapes),
        in_specs=[pl.BlockSpec(memory_space=pltpu.VMEM)] * 4,
        out_specs=(hbm,) * 4,
        scratch_shapes=[pltpu.SemaphoreType.DMA((4,))],
        name="hand_over",
    )(*[pltpu.with_memory_space_constraint(a, pltpu.VMEM) for a in out])


def solution(mesh):
    placed = (
        P("gr", "gc"),
        P("gr"),
        P("gc"),
        P(),
        P(),
        P(("gr", "gc"), None),
        P(("gr", "gc"), None),
        P(("gc", "gr"), None),
        P(("gc", "gr"), None),
    )
    return jax.shard_map(
        local,
        mesh=mesh,
        in_specs=placed,
        out_specs=(
            P(("gr", "gc"), None),
            P(("gr", "gc"), None),
            P(("gc", "gr"), None),
            P(("gc", "gr"), None),
        ),
        check_vma=False,
    )
```

```python
import functools

import jax
import jax.numpy as jnp
from jax import lax
from jax.experimental import pallas as pl
from jax.experimental.pallas import tpu as pltpu
from jax.sharding import PartitionSpec as P

F32 = jnp.float32
BF16 = jnp.bfloat16
MESH = pl.DeviceIdType.MESH

LEARN_RATE = 0.5
K = 256
NX, NZL = 4, 2
NZH, NY, NC = 4, 4, 2
RB = 160
CB = 64
XB = RB * NZL
QB = NY * NC * CB
ROWS = NX * XB
COLS = NZH * QB
SUB = 16
TILES = (
    (0, 0), (3, 0), (1, 0), (2, 0), (0, 1), (3, 1), (1, 1), (2, 1),
    (0, 2), (3, 2), (1, 2), (2, 2), (2, 3), (1, 3), (3, 3), (0, 3),
)
LATE = (1, 3, 4, 8, 12)
SPREAD = {1: 2, 2: 3}
FORWARD = {3: (1,), 6: (2,), 9: (3,)}
PIECES = (2, 1, 3, 0)
N_SEMS = 80


def lookup(table, ids):
    high = lax.shift_right_logical(ids, 7)
    low = ids & 127
    n_high, n = table.shape[0], ids.shape[1]
    hot = (lax.broadcasted_iota(jnp.int32, (n_high, n), 0) == high).astype(F32).astype(BF16)
    digits = [
        lax.shift_right_logical(table, 16),
        lax.shift_right_logical(table, 8) & 255,
        table & 255,
    ]
    parts = [
        jnp.dot(d.astype(F32).T.astype(BF16), hot, preferred_element_type=F32) for d in digits
    ]
    whole = parts[0] * 65536.0 + parts[1] * 256.0 + parts[2]
    mine = lax.broadcasted_iota(jnp.int32, (128, n), 0) == low
    return jnp.log(jnp.sum(jnp.where(mine, whole, 0.0), axis=0, keepdims=True))


def kernel(
    cnt_hbm, rid_hbm, cid_hbm, rmar_hbm, cmar_hbm, remb_hbm, racc_hbm, cemb_hbm, cacc_hbm,
    rnew_ref, raccn_ref, cnew_ref, caccn_ref,
    cnt, rid, cid, rmar, cmar, remb, racc, cemb, cacc,
    rows, rows_t, cols, row_term, col_term,
    s_ref, g_ref, row_part, col_tmp, col_part,
    ex_s, ex_r, col_s, y_r, z_s, z_r, row_s, row_r, w_s, w_r,
    local_sem, send_sem, recv_sem, z_send, z_recv, sum_send, sum_recv, here,
):
    gr = lax.axis_index("gr")
    gc = lax.axis_index("gc")
    c = lax.rem(gr, NC)
    y = lax.rem(gr // NC, NY)
    zh = gr // (NC * NY)
    zl = lax.rem(gc, NZL)
    x = gc // NZL

    def at(dx=0, dzl=0, dzh=0, dy=0, dc=0):
        g = (lax.rem(zh + dzh, NZH) * NY + lax.rem(y + dy, NY)) * NC + lax.rem(c + dc, NC)
        k = lax.rem(x + dx, NX) * NZL + lax.rem(zl + dzl, NZL)
        return (g, k)

    XP, XM, CO, LO = at(dx=1), at(dx=3), at(dc=1), at(dzl=1)
    neighbours = [at(dy=d) for d in (2, 1, 3)] + [at(dx=2), XP, XM, LO, CO]

    def z_device(to):
        return ((to * NY + y) * NC + c, gc)

    place = [zh] + [jnp.where(zh <= i, i + 1, i) for i in range(NZH - 1)]

    loads = []

    def load(src, dst):
        cp = pltpu.make_async_copy(src, dst, local_sem.at[len(loads)])
        cp.start()
        loads.append(cp)
        return cp

    l_remb, l_cemb = load(remb_hbm, remb), load(cemb_hbm, cemb)
    barrier = pltpu.get_barrier_semaphore()
    for n in neighbours:
        pl.semaphore_signal(barrier, inc=1, device_id=n, device_id_type=MESH)
    for to in range(1, NZH):

        @pl.when(zh < to)
        def _(to=to):
            pl.semaphore_signal(barrier, inc=1, device_id=z_device(to), device_id_type=MESH)

    l_ids = [load(rid_hbm, rid), load(cid_hbm, cid), load(rmar_hbm, rmar), load(cmar_hbm, cmar)]
    l_acc = [load(racc_hbm, racc), load(cacc_hbm, cacc)]

    copies = []

    def send(src, dst, target):
        i = len(copies)
        cp = pltpu.make_async_remote_copy(
            src_ref=src, dst_ref=dst, send_sem=send_sem.at[i], recv_sem=recv_sem.at[i],
            device_id=target, device_id_type=MESH,
        )
        cp.start()
        copies.append(cp)
        return cp

    def yy(d):
        return lax.rem(y + d, NY)

    def xx(d):
        return lax.rem(x + d, NX)

    def same(ref, target):
        return send(ref, ref, target)

    l_remb.wait()
    rows[x, zl] = (remb[...] * 0.5).astype(BF16)
    l_cemb.wait()
    cols[zh, y, c] = cemb[...].astype(BF16)
    pl.semaphore_wait(barrier, len(neighbours) + zh)

    own_r, own_c = rows.at[x, zl], cols.at[zh, y, c]
    y_in, core_in = {}, {}

    def z_copy(to):
        return pltpu.make_async_remote_copy(
            src_ref=own_c, dst_ref=own_c, send_sem=z_send.at[to], recv_sem=z_recv.at[zh],
            device_id=z_device(to), device_id_type=MESH,
        )

    for to in range(NZH - 1):

        @pl.when(zh > to)
        def _(to=to):
            pl.semaphore_signal(
                here.at[zh], inc=1, device_id=z_device(to), device_id_type=MESH
            )
            z_copy(to).start()

    def spread(b):
        piece = cols.at[place[b], y, c]
        if b:
            pltpu.make_async_remote_copy(
                src_ref=piece, dst_ref=piece, send_sem=z_send.at[place[b]],
                recv_sem=z_recv.at[place[b]], device_id=z_device(place[b]), device_id_type=MESH,
            ).wait_recv()
        core_in[b, 0] = same(piece, CO)
        for d in (2, 1, 3):
            y_in[b, d] = same(piece, at(dy=d))

    def cols_to_core(b):
        for d in (1, 3, 2):
            y_in[b, d].wait_recv()
            core_in[b, d] = same(cols.at[place[b], yy(NY - d), c], CO)

    spread(0)
    r_lo = same(own_r, LO)
    r_p0, r_m0, r_x2 = same(own_r, XP), same(own_r, XM), same(own_r, at(dx=2))

    l_cnt = [
        load(cnt_hbm.at[pl.ds(i * XB, XB)], cnt.at[pl.ds(i * XB, XB)]) for i in range(NX)
    ]
    for cp in l_ids:
        cp.wait()
    col_log = lookup(cmar[...], cid[...])
    col_term[...] = jnp.broadcast_to(0.5 * col_log, col_term.shape)
    r_lo.wait_recv()
    other_r = rows.at[x, 1 - zl]
    r_p1, r_m1 = same(other_r, XP), same(other_r, XM)
    for to in range(1, NZH):

        @pl.when(zh < to)
        def _(to=to):
            pl.semaphore_wait(here.at[to], 1)
            z_copy(to).start()

    spread(1)
    r_x2.wait_recv()
    r_lo2 = same(rows.at[xx(2), zl], LO)
    cols_to_core(0)
    row_log = lookup(rmar[...], rid[...].reshape(1, ROWS))
    log_total = jnp.log(jnp.sum(rmar[...].astype(F32)))
    row_vec = 0.5 * (row_log - log_total)
    for b in range(ROWS // 128):
        piece = jnp.broadcast_to(row_vec[:, b * 128 : (b + 1) * 128], (128, 128))
        row_term[b * 128 : (b + 1) * 128, :] = piece.T
    def rows_ready(dx):
        rows_t[:, dx * XB : (dx + 1) * XB] = rows[xx(dx)].reshape(XB, K).T

    def cols_ready(b):
        for d in range(NY):
            core_in[b, d].wait_recv()

    def before(t):
        dx, e = TILES[t]
        if t in SPREAD:
            spread(SPREAD[t])
        for b in FORWARD.get(t, ()):
            cols_to_core(b)
        if dx not in [a for a, _ in TILES[:t]]:
            for cp in {0: (), 1: (r_m0, r_m1), 2: (r_lo2,), 3: (r_p0, r_p1)}[dx]:
                cp.wait_recv()
            rows_ready(dx)
        if e not in [a for _, a in TILES[:t]]:
            cols_ready(e)
        if t == 0:
            for cp in l_cnt:
                cp.wait()

    def score(t):
        dx, e = TILES[t]
        s_ref[t % 2] = jnp.dot(
            rows[xx(dx)].reshape(XB, K), cols[place[e]].reshape(QB, K).T, preferred_element_type=F32
        )

    def elem(t):
        dx, e = TILES[t]
        r_at = pl.multiple_of(xx(dx) * XB, XB)
        for z in range(QB // 128):
            c_at = pl.multiple_of(place[e] * QB + z * 128, 128)
            c_row = col_term[:, pl.ds(c_at, 128)]
            for u in range(XB // SUB):
                at_u = pl.ds(pl.multiple_of(r_at + u * SUB, SUB), SUB)
                n = cnt[at_u, pl.ds(c_at, 128)]
                m = jnp.maximum(n, 1).astype(F32)
                inv = lax.rsqrt(m)
                half = (
                    s_ref[t % 2, u * SUB : (u + 1) * SUB, z * 128 : (z + 1) * 128] + jnp.log(inv)
                ) + (row_term[at_u, :] + c_row)
                g = jnp.where(n > 0, (m * inv + 0.4) * half, jnp.tanh(half) + 1.0)
                at_g = dx * XB + u * SUB
                g_ref[e, at_g : at_g + SUB, z * 128 : (z + 1) * 128] = g.astype(BF16)

    def row_grad(t):
        dx, e = TILES[t]
        part = jnp.dot(
            g_ref[e, dx * XB : (dx + 1) * XB, :],
            cols[place[e]].reshape(QB, K),
            preferred_element_type=F32,
        ).reshape(NZL, RB, K)
        if dx not in [a for a, _ in TILES[:t]]:
            row_part[dx] = part
        else:
            row_part[dx] += part

    ex, row_in = {}, {}

    def col_grad(e):
        t = jnp.dot(rows_t[...], g_ref[e], preferred_element_type=F32)
        col_tmp[e] = t.T.reshape(NY, NC, CB, K)
        for d in PIECES:
            ex_s[e, yy(d)] = col_tmp[e, yy(d), 1 - c].astype(BF16)
            ex[e, d] = send(ex_s.at[e, yy(d)], ex_r.at[e, yy(d)], CO)

    y_back, z_back = {}, {}

    def both_cores(e, d):
        ex[e, d].wait_recv()
        return col_tmp[e, yy(d), c] + ex_r[e, yy(d)].astype(F32)

    def col_out(e):
        for d in PIECES:
            if d:
                col_s[e, d - 1] = both_cores(e, d).astype(BF16)
                y_back[e, d] = send(col_s.at[e, d - 1], y_r.at[e, d - 1], at(dy=d))
            else:
                col_part[e] = both_cores(e, d)

    def sum_copy(e):
        return pltpu.make_async_remote_copy(
            src_ref=z_s.at[e - 1], dst_ref=z_r.at[zh], send_sem=sum_send.at[e],
            recv_sem=sum_recv.at[zh], device_id=z_device(place[e]), device_id_type=MESH,
        )

    def sum_in(e):
        pltpu.make_async_remote_copy(
            src_ref=z_s.at[e - 1], dst_ref=z_r.at[place[e]], send_sem=sum_send.at[e],
            recv_sem=sum_recv.at[place[e]], device_id=z_device(place[e]), device_id_type=MESH,
        ).wait_recv()

    def col_sum(e):
        total = col_part[e]
        for d in (1, 3, 2):
            y_back[e, d].wait_recv()
            total = total + y_r[e, d - 1].astype(F32)
        if e:
            z_s[e - 1] = total.astype(BF16)
            z_back[e] = sum_copy(e)
            z_back[e].start()
        else:
            col_part[0] = total

    def row_out(dx):
        for p in (1, 0):
            at_zl = lax.rem(zl + p, NZL)
            row_s[dx - 1, at_zl] = row_part[dx, at_zl].astype(BF16)
            row_in[dx, p] = send(row_s.at[dx - 1, at_zl], row_r.at[dx - 1, at_zl], at(dx=dx))

    n_tiles = len(TILES)
    row_end = {dx: max(i for i in range(n_tiles) if TILES[i][0] == dx) for dx in range(NX)}
    col_end = {e: max(i for i in range(n_tiles) if TILES[i][1] == e) for e in range(NZH)}
    col_order = sorted(range(NZH), key=col_end.get)
    for t in range(n_tiles + 2):
        late = t in LATE
        if t < n_tiles and not late:
            before(t)
            score(t)
        if 1 <= t <= n_tiles:
            elem(t - 1)
        if t >= 2:
            row_grad(t - 2)
        if late:
            before(t)
            score(t)
        for dx in range(1, NX):
            if t == row_end[dx] + 2:
                row_out(dx)
        for e in range(NZH):
            if t == col_end[e] + 2:
                col_grad(e)
        for e in col_order:
            if t == col_end[e] + 4:
                col_out(e)
            if t == col_end[e] + 10:
                col_sum(e)

    for e in col_order:
        if col_end[e] + 4 >= n_tiles + 2:
            col_out(e)
    left = [e for e in col_order if col_end[e] + 10 >= n_tiles + 2]
    for e in left[:-1]:
        col_sum(e)

    def row_sum(at_zl):
        total = row_part[0, at_zl]
        for i in range(NX - 1):
            total = total + row_r[i, at_zl].astype(F32)
        return total

    for dx in sorted((1, 2, 3), key=row_end.get):
        row_in[dx, 1].wait_recv()
    w_s[...] = row_sum(1 - zl).astype(BF16)
    w = send(w_s, w_r, LO)
    for e in left[-1:]:
        col_sum(e)
    for dx in (1, 3, 2):
        row_in[dx, 0].wait_recv()
    own = row_sum(zl)
    for cp in l_acc:
        cp.wait()

    def update(emb, acc, grad, new_ref, acc_ref):
        acc_new = acc + grad * grad
        acc_ref[...] = acc_new
        new_ref[...] = emb - LEARN_RATE * grad / jnp.sqrt(acc_new)

    w.wait_recv()
    update(remb[...], racc[...], (own + w_r[...].astype(F32)) * (1 / 256), rnew_ref, raccn_ref)
    total = col_part[0]
    for e in (1, 2, 3):
        sum_in(e)
        total = total + z_r[place[e]].astype(F32)
    update(cemb[...], cacc[...], total * (1 / 128), cnew_ref, caccn_ref)
    for cp in copies:
        cp.wait_send()
    for e in range(1, NZH):
        z_back[e].wait_send()
        z_copy(place[e]).wait_send()


def hand_over(*refs):
    n = len(refs) // 2
    sem = refs[-1]
    moves = [pltpu.make_async_copy(refs[i], refs[n + i], sem.at[i]) for i in range(n)]
    for m in moves:
        m.start()
    for m in moves:
        m.wait()


def local(counts, row_ids, col_ids, row_marginal, col_marginal, row_emb, row_acc, col_emb, col_acc):
    hbm = pl.BlockSpec(memory_space=pltpu.HBM)
    vmem = pltpu.VMEM
    i32 = jnp.int32
    scratch = [
        vmem((ROWS, COLS), i32), vmem((ROWS,), i32), vmem((1, COLS), i32),
        vmem((320, 128), i32), vmem((128, 128), i32),
        vmem((RB, K), F32), vmem((RB, K), F32), vmem((CB, K), F32), vmem((CB, K), F32),
        vmem((NX, NZL, RB, K), BF16), vmem((K, ROWS), BF16),
        vmem((NZH, NY, NC, CB, K), BF16),
        vmem((ROWS, 128), F32), vmem((SUB, COLS), F32),
        vmem((2, XB, QB), F32), vmem((NZH, ROWS, QB), BF16),
        vmem((NX, NZL, RB, K), F32), vmem((NZH, NY, NC, CB, K), F32), vmem((NZH, CB, K), F32),
        vmem((NZH, NY, CB, K), BF16), vmem((NZH, NY, CB, K), BF16),
        vmem((NZH, NY - 1, CB, K), BF16), vmem((NZH, NY - 1, CB, K), BF16),
        vmem((NZH - 1, CB, K), BF16), vmem((NZH, CB, K), BF16),
        vmem((NX - 1, NZL, RB, K), BF16), vmem((NX - 1, NZL, RB, K), BF16),
        vmem((RB, K), BF16), vmem((RB, K), BF16),
        pltpu.SemaphoreType.DMA((12,)),
        pltpu.SemaphoreType.DMA((N_SEMS,)),
        pltpu.SemaphoreType.DMA((N_SEMS,)),
        pltpu.SemaphoreType.DMA((NZH,)),
        pltpu.SemaphoreType.DMA((NZH,)),
        pltpu.SemaphoreType.DMA((NZH,)),
        pltpu.SemaphoreType.DMA((NZH,)),
        pltpu.SemaphoreType.REGULAR((NZH,)),
    ]
    shapes = ((RB, K), (RB, K), (CB, K), (CB, K))
    operands = (
        counts, row_ids, col_ids.reshape(1, COLS),
        row_marginal.reshape(320, 128), col_marginal.reshape(128, 128),
        row_emb, row_acc, col_emb, col_acc,
    )
    out = pl.pallas_call(
        kernel,
        out_shape=tuple(pltpu.VMEM(s, F32) for s in shapes),
        in_specs=[hbm] * 9,
        out_specs=(pl.BlockSpec(memory_space=pltpu.VMEM),) * 4,
        scratch_shapes=scratch,
        compiler_params=pltpu.CompilerParams(
            collective_id=0, has_side_effects=True, vmem_limit_bytes=48 * 1024 * 1024
        ),
        name="step",
    )(*[pltpu.with_memory_space_constraint(a, pltpu.HBM) for a in operands])
    return pl.pallas_call(
        hand_over,
        out_shape=tuple(jax.ShapeDtypeStruct(s, F32) for s in shapes),
        in_specs=[pl.BlockSpec(memory_space=pltpu.VMEM)] * 4,
        out_specs=(hbm,) * 4,
        scratch_shapes=[pltpu.SemaphoreType.DMA((4,))],
        name="hand_over",
    )(*[pltpu.with_memory_space_constraint(a, pltpu.VMEM) for a in out])


def solution(mesh):
    placed = (
        P("gr", "gc"),
        P("gr"),
        P("gc"),
        P(),
        P(),
        P(("gr", "gc"), None),
        P(("gr", "gc"), None),
        P(("gc", "gr"), None),
        P(("gc", "gr"), None),
    )
    return jax.shard_map(
        local,
        mesh=mesh,
        in_specs=placed,
        out_specs=(
            P(("gr", "gc"), None),
            P(("gr", "gc"), None),
            P(("gc", "gr"), None),
            P(("gc", "gr"), None),
        ),
        check_vma=False,
    )
```
